32 devices in a mesh: inst: 4 (over x, core), blk: 8 (over z, y).
Axes of the slice: x: 2, y: 2, z: 4, core: 2. Of those that a mesh axis runs over, the one named last changes fastest.
Arguments:
- state: float32 [4, 2, 6, 8, 8, 1024], P('inst', None, None, None, None, 'blk'), may hold values from -0.5 to 3, as said below
- donor_block: int32 [4, 2, 8], P('inst', None, 'blk'), may hold values from 0 to 7, as said below
- donor_offset: int32 [4, 2, 8], P('inst', None, 'blk'), may hold values from 0 to 127, as said below
Outputs:
- hb_residual: float32 [4, 2, 6, 8, 8, 1024], P('inst', None, None, None, None, 'blk')
- new_state: float32 [4, 2, 6, 8, 8, 1024], P('inst', None, None, None, None, 'blk')
The draws below stay inside these ranges and needn't reach their ends.
Inputs may be any that keep to these rules, and one draw needn't show every extreme that they name: For each instance n and row r there is one rotation R with donor_block[n, r, b] = (b + R) mod 8 for every block b. `donor_offset`: for each instance and row the offset is the same for all blocks. `state`: density lies in [0.8, 1.25], momenta in [-0.5, 0.5], total energy in [2, 3], turbulence variable in [0.05, 0.5].
All inputs are finite; a program needn't handle non-finite values.
Results may differ from the reference program's by a relative error of at most 0.0003.
Values sent between devices are 32-bit elements; how exact they have to be, the bound alone decides.
A program may use at most 64 MiB of HBM per device.

```python
import jax
import jax.numpy as jnp
from jax import lax

CI = 8
CJ = 8
CK = 128
INSTANCES = 4
NBLOCKS = 8


def draw_state(key, part):
    cell_shape = (INSTANCES, 2, 6, CI, CJ, CK * NBLOCKS)
    low_end = jnp.array([0.8, -0.5, -0.5, -0.5, 2.0, 0.05], jnp.float32).reshape(1, 1, 6, 1, 1, 1)
    high_end = jnp.array([1.25, 0.5, 0.5, 0.5, 3.0, 0.5], jnp.float32).reshape(1, 1, 6, 1, 1, 1)
    uniform_part = jax.random.uniform(key, cell_shape, jnp.float32)
    return low_end + (high_end - low_end) * uniform_part


def draw_donor_block(key, part):
    rotations = jax.random.randint(jax.random.fold_in(key, 11), (INSTANCES, 2, 1), 0, NBLOCKS)
    sectors = jnp.arange(NBLOCKS, dtype=jnp.int32).reshape(1, 1, NBLOCKS)
    return jnp.mod(sectors + rotations, NBLOCKS).astype(jnp.int32)


def draw_donor_offset(key, part):
    offsets = jax.random.randint(jax.random.fold_in(key, 13), (INSTANCES, 2, 1), 0, CK)
    offsets = offsets.at[0, 0, 0].set(CK - 1)
    offsets = offsets.at[0, 1, 0].set(0)
    return jnp.broadcast_to(offsets, (INSTANCES, 2, NBLOCKS)).astype(jnp.int32)


def setup_inputs(seed: int = 0) -> dict:
    streams_of = jax.random.split(jax.random.key(seed), 4)
    return {
        "state": draw_state(jax.random.fold_in(streams_of[3], 71), 0),
        "donor_block": draw_donor_block(jax.random.fold_in(streams_of[3], 71), 0),
        "donor_offset": draw_donor_offset(jax.random.fold_in(streams_of[3], 71), 0),
    }


gamma_ratio = 1.4
second_coef = 0.5
fourth_coef = 1.0 / 32.0
courant = 0.8
frequency = 0.5
highest = lax.Precision.HIGHEST

def spectral_weights(target, source, number):
    distance = jnp.mod(target - source, number)
    angle = jnp.pi / number * distance.astype(jnp.float32)
    parity = 1.0 - 2.0 * jnp.mod(distance, 2).astype(jnp.float32)
    nonzero = distance != 0
    sine_safe = jnp.where(nonzero, jnp.sin(angle), 1.0)
    cotangent = jnp.where(nonzero, jnp.cos(angle) / sine_safe, 0.0)
    return parity * (0.25 * frequency + 0.5 * frequency * cotangent)

def take_range(array, begin, length, along):
    return lax.slice_in_dim(array, begin, begin + length, axis=along)

def flux_divergence(extended, along):
    length = extended.shape[along] - 4
    cell_axis = along - 1
    density = extended[0]
    inverse = 1.0 / density
    normal_vel = extended[along] * inverse
    kinetic = 0.5 * (extended[1] ** 2 + extended[2] ** 2 + extended[3] ** 2) * inverse
    pressure = (gamma_ratio - 1.0) * (extended[4] - kinetic)
    sound = jnp.sqrt(gamma_ratio * pressure * inverse)
    momentum_flux = []
    for component in (1, 2, 3):
        if component == along:
            momentum_flux.append(extended[component] * normal_vel + pressure)
        else:
            momentum_flux.append(extended[component] * normal_vel)
    fluxes = jnp.stack([extended[along]] + momentum_flux + [(extended[4] + pressure) * normal_vel, extended[5] * normal_vel])
    radius = jnp.abs(normal_vel) + sound
    p_plus = take_range(pressure, 2, length + 2, cell_axis)
    p_here = take_range(pressure, 1, length + 2, cell_axis)
    p_minus = take_range(pressure, 0, length + 2, cell_axis)
    sensor = jnp.abs(p_plus - 2.0 * p_here + p_minus) / (p_plus + 2.0 * p_here + p_minus)
    spread = 0.5 * (take_range(radius, 1, length + 1, cell_axis) + take_range(radius, 2, length + 1, cell_axis))
    eps_two = second_coef * jnp.maximum(take_range(sensor, 0, length + 1, cell_axis), take_range(sensor, 1, length + 1, cell_axis))
    eps_four = jnp.maximum(0.0, fourth_coef - eps_two)
    first_diff = take_range(extended, 2, length + 1, along) - take_range(extended, 1, length + 1, along)
    third_diff = take_range(extended, 3, length + 1, along) - 3.0 * take_range(extended, 2, length + 1, along) + 3.0 * take_range(extended, 1, length + 1, along) - take_range(extended, 0, length + 1, along)
    interface = 0.5 * (take_range(fluxes, 1, length + 1, along) + take_range(fluxes, 2, length + 1, along)) - spread * (eps_two * first_diff - eps_four * third_diff)
    return take_range(interface, 1, length, along) - take_range(interface, 0, length, along)

def wall_extend(block):
    mirror_sign = jnp.array([1.0, 1.0, -1.0, 1.0, 1.0, 1.0], jnp.float32).reshape(6, 1, 1, 1)
    lower_ghost = block[:, :, 0:2][:, :, ::-1] * mirror_sign
    upper_ghost = block[:, :, -2:][:, :, ::-1] * mirror_sign
    return jnp.concatenate([lower_ghost, block, upper_ghost], axis=2)

def row_residual(block, low_ghost, high_ghost, circum_ext):
    axial_ext = jnp.concatenate([low_ghost, block, high_ghost], axis=1)
    return flux_divergence(axial_ext, 1) + flux_divergence(wall_extend(block), 2) + flux_divergence(circum_ext, 3)

def local_step(fields, number):
    inverse = 1.0 / fields[:, 0]
    kinetic = 0.5 * (fields[:, 1] ** 2 + fields[:, 2] ** 2 + fields[:, 3] ** 2) * inverse
    pressure = (gamma_ratio - 1.0) * (fields[:, 4] - kinetic)
    sound = jnp.sqrt(gamma_ratio * pressure * inverse)
    speeds = (jnp.abs(fields[:, 1]) + jnp.abs(fields[:, 2]) + jnp.abs(fields[:, 3])) * inverse
    return courant / (speeds + 3.0 * sound + frequency * number / 2.0)

def periodic(field_block):
    return jnp.concatenate([field_block[..., -2:], field_block, field_block[..., :2]], axis=-1)

def reference(state, donor_block, donor_offset):
    number = state.shape[0]
    indices = jnp.arange(number, dtype=jnp.int32)
    matrix = spectral_weights(indices[:, None], indices[None, :], number)
    spectral = jnp.tensordot(matrix, state, axes=(1, 0), precision=highest)

    def one_instance(packed):
        fields, time_term, blocks_of, offsets_of = packed
        rotor = fields[0]
        stator = fields[1]
        total_k = rotor.shape[3]
        positions = jnp.arange(total_k, dtype=jnp.int32)
        owner = positions // CK
        local_pos = jnp.mod(positions, CK)
        rotor_index = jnp.mod(jnp.take(blocks_of[0], owner) * CK + jnp.take(offsets_of[0], owner) + local_pos, total_k).astype(jnp.int32)
        stator_index = jnp.mod(jnp.take(blocks_of[1], owner) * CK + jnp.take(offsets_of[1], owner) + local_pos, total_k).astype(jnp.int32)
        rotor_high = jnp.take(stator[:, 0:2], rotor_index, axis=3)
        stator_low = jnp.take(rotor[:, -2:], stator_index, axis=3)
        rotor_low = jnp.concatenate([rotor[:, 0:1], rotor[:, 0:1]], axis=1)
        stator_high = jnp.concatenate([stator[:, -1:], stator[:, -1:]], axis=1)
        rotor_res = row_residual(rotor, rotor_low, rotor_high, periodic(rotor))
        stator_res = row_residual(stator, stator_low, stator_high, periodic(stator))
        residual = jnp.stack([rotor_res, stator_res]) + time_term
        step = local_step(fields, number)
        return (residual, fields - step[:, None] * residual)
    return lax.map(one_instance, (state, spectral, donor_block, donor_offset))
```

```python
import functools
import math

import jax
import jax.numpy as jnp
from jax import lax
from jax.experimental import pallas as pl
from jax.experimental.pallas import tpu as pltpu
from jax.sharding import PartitionSpec as P

GAMMA = 1.4
K2 = 0.5
K4 = 1.0 / 32.0
COURANT = 0.8
FREQ = 0.5
GROUP = 2
MESH = pl.DeviceIdType.MESH
f32 = jnp.float32


def spectral_constants(number):
    out = []
    for r in range(number):
        cot = 0.0 if r == 0 else math.cos(math.pi * r / number) / math.sin(math.pi * r / number)
        out.append((-1.0) ** r * (0.25 * FREQ + 0.5 * FREQ * cot))
    return out


def primitives(e):
    inverse = 1.0 / e[0]
    kinetic = 0.5 * (e[1] * e[1] + e[2] * e[2] + e[3] * e[3]) * inverse
    pressure = (GAMMA - 1.0) * (e[4] - kinetic)
    sound = jnp.sqrt(GAMMA * pressure * inverse)
    return inverse, pressure, sound


def fluxes(e, a, inverse, pressure):
    u = e[a] * inverse
    out = [e[a]]
    for k in (1, 2, 3):
        out.append(e[k] * u + pressure if k == a else e[k] * u)
    return u, out + [(e[4] + pressure) * u, e[5] * u]


def sensor(minus, here, plus):
    total = plus + minus
    return jnp.abs(total - 2.0 * here) / (total + 2.0 * here)


def weights_of(nu0, nu1, lam0, lam1):
    spread = 0.5 * (lam0 + lam1)
    eps2 = K2 * jnp.maximum(nu0, nu1)
    eps4 = jnp.maximum(0.0, K4 - eps2)
    fourth = spread * eps4
    return spread * eps2 + 3.0 * fourth, fourth


def face(flux0, flux1, first, fourth, em, e0, e1, e2):
    return 0.5 * (flux0 + flux1) - first * (e1 - e0) + fourth * (e2 - em)


def circumferential(e, inverse, pressure, sound):
    axis = e[0].ndim - 1

    def nxt(v):
        return pltpu.roll(v, 127, axis)

    def prv(v):
        return pltpu.roll(v, 1, axis)

    u, flux = fluxes(e, 3, inverse, pressure)
    lam = jnp.abs(u) + sound
    nu = sensor(prv(pressure), pressure, nxt(pressure))
    first, fourth = weights_of(nu, nxt(nu), lam, nxt(lam))
    out = []
    for k in range(6):
        e1 = nxt(e[k])
        h = face(flux[k], nxt(flux[k]), first, fourth, prv(e[k]), e[k], e1, nxt(e1))
        out.append(h - prv(h))
    return out


def radial(e, inverse, pressure, sound):
    axis = e[0].ndim - 2
    row = lax.broadcasted_iota(jnp.int32, e[0].shape, axis)
    top, bottom = row == 7, row == 0

    def nxt(v, s=1.0):
        return jnp.where(top, v if s > 0 else -v, pltpu.roll(v, 7, axis))

    def prv(v, s=1.0):
        return jnp.where(bottom, v if s > 0 else -v, pltpu.roll(v, 1, axis))

    u, flux = fluxes(e, 2, inverse, pressure)
    lam = jnp.abs(u) + sound
    nu = sensor(prv(pressure), pressure, nxt(pressure))
    first, fourth = weights_of(nu, nxt(nu), lam, nxt(lam))
    out = []
    for k in range(6):
        s = -1.0 if k == 2 else 1.0
        e1 = nxt(e[k], s)
        em = prv(e[k], s)
        e2 = jnp.where(top, em if s > 0 else -em, pltpu.roll(e1, 7, axis))
        h = face(flux[k], nxt(flux[k], -s), first, fourth, em, e[k], e1, e2)
        if k == 2:
            eps2 = K2 * nu
            eps4 = jnp.maximum(0.0, K4 - eps2)
            wall = flux[2] - lam * (eps2 * (2.0 * e[2]) - eps4 * (2.0 * e1 - 6.0 * e[2]))
        else:
            wall = jnp.zeros_like(h)
        out.append(h - jnp.where(bottom, wall, pltpu.roll(h, 1, axis)))
    return out


def kernel(
    number,
    blocks,
    db_ref,
    do_ref,
    st_ref,
    res_ref,
    new_ref,
    own,
    inv,
    prs,
    snd,
    buf,
    fx,
    hx,
    step,
    faces_out,
    faces_in,
    stage,
    yrecv,
    pk,
    pkl,
    pkr,
    edge,
    own_sem,
    face_sem,
    x_send,
    x_recv,
    c_send,
    c_recv,
    f_send,
    f_recv,
    up_send,
    up_recv,
    dn_send,
    dn_recv,
    y_send,
    y_recv,
    g_send,
    g_recv,
):
    faces = (faces_out, faces_in)
    n = lax.axis_index("inst")
    b = lax.axis_index("blk")
    pairs = number // 2
    depth = blocks // 2
    ups = depth // 2
    downs = depth - 1 - ups
    pair, core = n // 2, n % 2
    z, y = b // 2, b % 2
    partner = n + 1 - 2 * core
    ypartner = b + 1 - 2 * y
    zup = lax.rem(z + 1, depth)
    zdown = lax.rem(z + depth - 1, depth)
    bright = lax.rem(b + 1, blocks)
    bleft = lax.rem(b + blocks - 1, blocks)
    chunks = [(r, f) for r in range(2) for f in range(0, 6, GROUP)]

    def peer(dp):
        return lax.rem(pair + dp, pairs) * 2 + core

    own_copy = pltpu.make_async_copy(st_ref.at[0], own.at[:, :, 2:10], own_sem)
    own_copy.start()

    def face_of(kind):
        return st_ref.at[0, 0, :, 6:8] if kind == 0 else st_ref.at[0, 1, :, 0:2]

    face_copies = []
    for kind in range(2):
        c = pltpu.make_async_copy(face_of(kind), faces[kind].at[z], face_sem.at[kind])
        c.start()
        face_copies.append(c)

    barrier = pltpu.get_barrier_semaphore()
    greet = [(peer(dp), b) for dp in range(1, pairs)]
    greet += [(partner, b), (n, ypartner), (n, bright), (n, bleft)]
    greet += [(n, zup * 2 + y), (n, zdown * 2 + y)]
    for target in greet:
        pl.semaphore_signal(barrier, inc=1, device_id=target, device_id_type=MESH)
    pl.semaphore_wait(barrier, len(greet))

    def remote(src, dst, ss, rs, target):
        return pltpu.make_async_remote_copy(
            src_ref=src, dst_ref=dst, send_sem=ss, recv_sem=rs, device_id=target, device_id_type=MESH
        )

    x_copies = []
    for ci, (r, f) in enumerate(chunks):
        for dp in range(1, pairs):
            c = remote(
                st_ref.at[0, r, f : f + GROUP],
                buf.at[n, r, f : f + GROUP],
                x_send.at[dp - 1, ci],
                x_recv.at[dp - 1, ci],
                (peer(dp), b),
            )
            c.start()
            x_copies.append(c)
    up_copies, dn_copies = {}, {}
    for kind in range(2):
        for s in range(ups):
            slot = lax.rem(z + depth - s, depth)
            src = face_of(kind) if s == 0 else faces[kind].at[slot]
            up_copies[kind, s] = remote(
                src, faces[kind].at[slot], up_send.at[kind, s], up_recv.at[kind, s], (n, zup * 2 + y)
            )
        for s in range(downs):
            slot = lax.rem(z + s, depth)
            src = face_of(kind) if s == 0 else faces[kind].at[slot]
            dn_copies[kind, s] = remote(
                src, faces[kind].at[slot], dn_send.at[kind, s], dn_recv.at[kind, s], (n, zdown * 2 + y)
            )
    for kind in range(2):
        up_copies[kind, 0].start()
        if downs:
            dn_copies[kind, 0].start()
    c_copies = []
    for r in range(2):
        c = remote(st_ref.at[0, r], buf.at[n, r], c_send.at[r], c_recv.at[r], (partner, b))
        c.start()
        c_copies.append(c)

    own_copy.wait()
    lane = lax.broadcasted_iota(jnp.int32, (8, 128), 1)
    group = lax.rem(lane + 2, 128) // 8
    for k in range(6):
        acc = jnp.zeros((8, 128), f32)
        for i in range(8):
            for r in range(2):
                t = 2 * i + r
                acc = jnp.where(group == t, pltpu.roll(own[r, k, 2 + i], (8 * t + 2) % 128, 1), acc)
        pk[k] = acc
    g_copies = [
        remote(pk, pkl, g_send.at[0], g_recv.at[0], (n, bright)),
        remote(pk, pkr, g_send.at[1], g_recv.at[1], (n, bleft)),
    ]
    for c in g_copies:
        c.start()

    lane3 = lax.broadcasted_iota(jnp.int32, (2, 8, 128), 2)
    inner = (lane3 >= 2) & (lane3 < 126)

    def body(i, carry):
        e = [own[:, k, 2 + i] for k in range(6)]
        inverse, pressure, sound = primitives(e)
        inv[:, 2 + i] = inverse
        prs[:, 2 + i] = pressure
        snd[:, 2 + i] = sound
        speeds = (jnp.abs(e[1]) + jnp.abs(e[2]) + jnp.abs(e[3])) * inverse
        step[:, i] = COURANT / (speeds + 3.0 * sound + FREQ * number / 2.0)
        d2 = radial(e, inverse, pressure, sound)
        d3 = circumferential(e, inverse, pressure, sound)
        for k in range(6):
            fx[:, k, i] = d2[k] + jnp.where(inner, d3[k], 0.0)
        return carry

    def ring(s):
        for kind in range(2):
            if s < ups:
                up_copies[kind, s - 1].wait_recv()
                up_copies[kind, s].start()
            if s < downs:
                dn_copies[kind, s - 1].wait_recv()
                dn_copies[kind, s].start()

    lax.fori_loop(0, 4, body, 0)
    for s in range(1, max(ups, downs)):
        ring(s)
    lax.fori_loop(4, 8, body, 0)

    for g in range(2):
        own[0, :, g] = own[0, :, 2]
        own[1, :, 10 + g] = own[1, :, 9]
        for ref in (inv, prs, snd):
            ref[0, g] = ref[0, 2]
            ref[1, 10 + g] = ref[1, 9]

    def axial(r, f):
        em, e0, e1, e2 = [[own[r, k, f + s] for k in range(6)] for s in range(4)]
        pm, p0, p1, p2 = [prs[r, f + s] for s in range(4)]
        u0, flux0 = fluxes(e0, 1, inv[r, f + 1], p0)
        u1, flux1 = fluxes(e1, 1, inv[r, f + 2], p1)
        first, fourth = weights_of(
            sensor(pm, p0, p1),
            sensor(p0, p1, p2),
            jnp.abs(u0) + snd[r, f + 1],
            jnp.abs(u1) + snd[r, f + 2],
        )
        for k in range(6):
            hx[r, k, f] = face(flux0[k], flux1[k], first, fourth, em[k], e0[k], e1[k], e2[k])

    def axial_body(f, carry):
        axial(0, f)
        axial(1, f + 2)
        return carry

    lax.fori_loop(0, 7, axial_body, 0)

    for c in g_copies:
        c.wait_recv()
    phase = lax.rem(lane, 8)
    strips = []
    for k in range(6):
        mine = pk[k]
        left = jnp.where(phase < 2, pkl[k], mine)
        right = jnp.where((phase >= 2) & (phase < 4), pkr[k], mine)
        strips.append(jnp.stack([left, right]))
    d3 = circumferential(strips, *primitives(strips))
    for k in range(6):
        edge[k] = jnp.where(phase < 2, d3[k][1], d3[k][0])
    outer = (lane < 2) | (lane >= 126)
    for k in range(6):
        both = edge[k]
        for i in range(8):
            for r in range(2):
                shift = (128 - (8 * (2 * i + r) + 2)) % 128
                fx[r, k, i] += jnp.where(outer, pltpu.roll(both, shift, 1), 0.0)

    for kind in range(2):
        face_copies[kind].wait()
    y_copies = []
    for kind in range(2):
        if ups:
            up_copies[kind, ups - 1].wait_recv()
        if downs:
            dn_copies[kind, downs - 1].wait_recv()
        row = 1 - kind
        donor = lax.rem(db_ref[0, row, 0] + (ypartner - b) + blocks, blocks)
        after = lax.rem(donor + 1, blocks)
        pick = jnp.where(lax.rem(donor, 2) == y, donor // 2, after // 2)
        stage[kind] = faces[kind][pick]
        c = remote(stage.at[kind], yrecv.at[kind], y_send.at[kind], y_recv.at[kind], (n, ypartner))
        c.start()
        y_copies.append(c)

    f_copies = {}

    def forward(ci):
        r, f = chunks[ci]
        for dp in range(1, pairs):
            x_copies[ci * (pairs - 1) + dp - 1].wait_recv()
            slot = lax.rem(pair + pairs - dp, pairs) * 2 + core
            ref = buf.at[slot, r, f : f + GROUP]
            f_copies[dp, ci] = remote(
                ref, ref, f_send.at[dp - 1, ci], f_recv.at[dp - 1, ci], (partner, b)
            )
            f_copies[dp, ci].start()

    early = len(chunks) - 2
    for ci in range(early):
        forward(ci)

    for kind in range(2):
        y_copies[kind].wait_recv()
        row = 1 - kind
        donor = db_ref[0, row, 0]
        offset = do_ref[0, row, 0]
        after = lax.rem(donor + 1, blocks)
        same = lax.rem(donor, 2) == y
        pick = jnp.where(same, donor // 2, after // 2)
        mask = (lane >= offset) == same
        shift = lax.rem(128 - offset, 128)
        base = 10 if row == 0 else 0
        for s in range(2):
            ghost = []
            for k in range(6):
                cells = jnp.where(mask, faces[kind][pick, k, s], yrecv[kind, k, s])
                ghost.append(pltpu.roll(cells, shift, 1))
                own[row, k, base + s] = ghost[k]
            inverse, pressure, sound = primitives(ghost)
            inv[row, base + s] = inverse
            prs[row, base + s] = pressure
            snd[row, base + s] = sound
    for s in range(2):
        axial(0, 7 + s)
        axial(1, s)

    for ci in range(early, len(chunks)):
        forward(ci)

    for r in range(2):
        c_copies[r].wait_recv()
    consts = spectral_constants(number)
    for ci, (r, f) in enumerate(chunks):
        for dp in range(1, pairs):
            f_copies[dp, ci].wait_recv()
        for k in range(f, f + GROUP):
            mine = own[r, k, 2:10]
            time = consts[0] * mine
            for q in range(1, number):
                time += consts[q] * buf[lax.rem(n + number - q, number), r, k]
            total = (hx[r, k, 1:9] - hx[r, k, 0:8]) + fx[r, k] + time
            res_ref[0, r, k] = total
            new_ref[0, r, k] = mine - step[r] * total

    for c in x_copies + c_copies + list(f_copies.values()) + g_copies + y_copies:
        c.wait_send()
    for c in list(up_copies.values()) + list(dn_copies.values()):
        c.wait_send()


def per_device(number, blocks, state, donor_block, donor_offset):
    pairs, depth = number // 2, blocks // 2
    ups = depth // 2
    downs = max(depth - 1 - ups, 1)
    nch = 2 * (6 // GROUP)
    dma = pltpu.SemaphoreType.DMA
    vmem = lambda *shape: pltpu.VMEM(shape, f32)
    shape = jax.ShapeDtypeStruct(state.shape, f32)
    return pl.pallas_call(
        functools.partial(kernel, number, blocks),
        out_shape=(shape, shape),
        in_specs=[
            pl.BlockSpec(memory_space=pltpu.SMEM),
            pl.BlockSpec(memory_space=pltpu.SMEM),
            pl.BlockSpec(memory_space=pl.ANY),
        ],
        out_specs=(
            pl.BlockSpec(memory_space=pltpu.VMEM),
            pl.BlockSpec(memory_space=pltpu.VMEM),
        ),
        scratch_shapes=[
            vmem(2, 6, 12, 8, 128),
            vmem(2, 12, 8, 128),
            vmem(2, 12, 8, 128),
            vmem(2, 12, 8, 128),
            vmem(number, 2, 6, 8, 8, 128),
            vmem(2, 6, 8, 8, 128),
            vmem(2, 6, 9, 8, 128),
            vmem(2, 8, 8, 128),
            vmem(depth, 6, 2, 8, 128),
            vmem(depth, 6, 2, 8, 128),
            vmem(2, 6, 2, 8, 128),
            vmem(2, 6, 2, 8, 128),
            vmem(6, 8, 128),
            vmem(6, 8, 128),
            vmem(6, 8, 128),
            vmem(6, 8, 128),
            dma,
            dma((2,)),
            dma((pairs, nch)),
            dma((pairs, nch)),
            dma((2,)),
            dma((2,)),
            dma((pairs, nch)),
            dma((pairs, nch)),
            dma((2, max(ups, 1))),
            dma((2, max(ups, 1))),
            dma((2, downs)),
            dma((2, downs)),
            dma((2,)),
            dma((2,)),
            dma((2,)),
            dma((2,)),
        ],
        compiler_params=pltpu.CompilerParams(
            collective_id=0, has_side_effects=True, vmem_limit_bytes=32 * 1024 * 1024
        ),
    )(donor_block, donor_offset, state)


def solution(mesh):
    number, blocks = mesh.shape["inst"], mesh.shape["blk"]
    return jax.shard_map(
        functools.partial(per_device, number, blocks),
        mesh=mesh,
        in_specs=(
            P("inst", None, None, None, None, "blk"),
            P("inst", None, "blk"),
            P("inst", None, "blk"),
        ),
        out_specs=(
            P("inst", None, None, None, None, "blk"),
            P("inst", None, None, None, None, "blk"),
        ),
        check_vma=False,
    )
```

```python
import functools
import math

import jax
import jax.numpy as jnp
from jax import lax
from jax.experimental import pallas as pl
from jax.experimental.pallas import tpu as pltpu
from jax.sharding import PartitionSpec as P

GAMMA = 1.4
K2 = 0.5
K4 = 1.0 / 32.0
COURANT = 0.8
FREQ = 0.5
GROUP = 2
RAW = 2
MESH = pl.DeviceIdType.MESH
f32 = jnp.float32


def spectral_constants(number):
    out = []
    for r in range(number):
        cot = 0.0 if r == 0 else math.cos(math.pi * r / number) / math.sin(math.pi * r / number)
        out.append((-1.0) ** r * (0.25 * FREQ + 0.5 * FREQ * cot))
    return out


def primitives(e):
    inverse = 1.0 / e[0]
    kinetic = 0.5 * (e[1] * e[1] + e[2] * e[2] + e[3] * e[3]) * inverse
    pressure = (GAMMA - 1.0) * (e[4] - kinetic)
    sound = jnp.sqrt(GAMMA * pressure * inverse)
    return inverse, pressure, sound


def fluxes(e, a, inverse, pressure):
    u = e[a] * inverse
    out = [e[a]]
    for k in (1, 2, 3):
        out.append(e[k] * u + pressure if k == a else e[k] * u)
    return u, out + [(e[4] + pressure) * u, e[5] * u]


def sensor(minus, here, plus):
    total = plus + minus
    return jnp.abs(total - 2.0 * here) / (total + 2.0 * here)


def weights_of(nu0, nu1, lam0, lam1):
    spread = 0.5 * (lam0 + lam1)
    eps2 = K2 * jnp.maximum(nu0, nu1)
    eps4 = jnp.maximum(0.0, K4 - eps2)
    fourth = spread * eps4
    return spread * eps2 + 3.0 * fourth, fourth


def face(flux0, flux1, first, fourth, em, e0, e1, e2):
    return 0.5 * (flux0 + flux1) - first * (e1 - e0) + fourth * (e2 - em)


def circumferential(e, inverse, pressure, sound):
    axis = e[0].ndim - 1

    def nxt(v):
        return pltpu.roll(v, 127, axis)

    def prv(v):
        return pltpu.roll(v, 1, axis)

    u, flux = fluxes(e, 3, inverse, pressure)
    lam = jnp.abs(u) + sound
    nu = sensor(prv(pressure), pressure, nxt(pressure))
    first, fourth = weights_of(nu, nxt(nu), lam, nxt(lam))
    out = []
    for k in range(6):
        e1 = nxt(e[k])
        h = face(flux[k], nxt(flux[k]), first, fourth, prv(e[k]), e[k], e1, nxt(e1))
        out.append(h - prv(h))
    return out


def radial(e, inverse, pressure, sound):
    axis = e[0].ndim - 2
    row = lax.broadcasted_iota(jnp.int32, e[0].shape, axis)
    top, bottom = row == 7, row == 0

    def nxt(v, s=1.0):
        return jnp.where(top, v if s > 0 else -v, pltpu.roll(v, 7, axis))

    def prv(v, s=1.0):
        return jnp.where(bottom, v if s > 0 else -v, pltpu.roll(v, 1, axis))

    u, flux = fluxes(e, 2, inverse, pressure)
    lam = jnp.abs(u) + sound
    nu = sensor(prv(pressure), pressure, nxt(pressure))
    first, fourth = weights_of(nu, nxt(nu), lam, nxt(lam))
    out = []
    for k in range(6):
        s = -1.0 if k == 2 else 1.0
        e1 = nxt(e[k], s)
        em = prv(e[k], s)
        e2 = jnp.where(top, em if s > 0 else -em, pltpu.roll(e1, 7, axis))
        h = face(flux[k], nxt(flux[k], -s), first, fourth, em, e[k], e1, e2)
        if k == 2:
            eps2 = K2 * nu
            eps4 = jnp.maximum(0.0, K4 - eps2)
            wall = flux[2] - lam * (eps2 * (2.0 * e[2]) - eps4 * (2.0 * e1 - 6.0 * e[2]))
        else:
            wall = jnp.zeros_like(h)
        out.append(h - jnp.where(bottom, wall, pltpu.roll(h, 1, axis)))
    return out


def kernel(
    number,
    blocks,
    db_ref,
    do_ref,
    st_ref,
    res_ref,
    new_ref,
    own,
    inv,
    prs,
    snd,
    buf,
    fx,
    hx,
    step,
    share,
    faces,
    merged,
    stage,
    yfirst,
    ylast,
    pk,
    pkl,
    pkr,
    edge,
    own_sem,
    face_sem,
    x_send,
    x_recv,
    c_send,
    c_recv,
    f_send,
    f_recv,
    z_send,
    z_recv,
    y_send,
    y_recv,
    g_send,
    g_recv,
):
    n = lax.axis_index("inst")
    b = lax.axis_index("blk")
    pairs = number // 2
    depth = blocks // 2
    pair, core = n // 2, n % 2
    z, y = b // 2, b % 2
    partner = n + 1 - 2 * core
    ypartner = b + 1 - 2 * y
    bright = lax.rem(b + 1, blocks)
    bleft = lax.rem(b + blocks - 1, blocks)
    chunks = [(r, f) for r in range(2) for f in range(0, 6, GROUP)]

    def peer(dp):
        return lax.rem(pair + dp, pairs) * 2 + core

    own_copy = pltpu.make_async_copy(st_ref.at[0], own.at[:, :, 2:10], own_sem)
    own_copy.start()
    outlet = st_ref.at[0, 0, :, 6:8]
    inlet = st_ref.at[0, 1, :, 0:2]
    face_copy = pltpu.make_async_copy(outlet, faces.at[z], face_sem)
    face_copy.start()

    def column(s):
        return (n, lax.rem(z + s, depth) * 2 + y)

    barrier = pltpu.get_barrier_semaphore()
    greet = [(peer(dp), b) for dp in range(1, pairs)]
    greet += [(partner, b), (n, ypartner), (n, bright), (n, bleft)]
    greet += [column(s) for s in range(1, depth)]
    for target in greet:
        pl.semaphore_signal(barrier, inc=1, device_id=target, device_id_type=MESH)
    pl.semaphore_wait(barrier, len(greet))

    def remote(src, dst, ss, rs, target):
        return pltpu.make_async_remote_copy(
            src_ref=src, dst_ref=dst, send_sem=ss, recv_sem=rs, device_id=target, device_id_type=MESH
        )

    x_copies, c_copies = {}, {}
    for ci, (r, f) in enumerate(chunks):
        part = (r, slice(f, f + GROUP))
        for dp in range(1, pairs):
            src = st_ref.at[(0, *part)] if ci < RAW else share.at[(dp - 1, *part)]
            x_copies[ci, dp] = remote(
                src,
                buf.at[(n, *part)],
                x_send.at[dp - 1, ci],
                x_recv.at[dp - 1, ci],
                (peer(dp), b),
            )
        c_copies[ci] = remote(
            st_ref.at[(0, *part)], buf.at[(n, *part)], c_send.at[ci], c_recv.at[ci], (partner, b)
        )
    for ci in range(RAW):
        for dp in range(1, pairs):
            x_copies[ci, dp].start()
    first_copy = remote(inlet, yfirst, y_send.at[1], y_recv.at[1], (n, ypartner))
    first_copy.start()
    for ci in list(range(RAW, len(chunks))) + list(range(RAW)):
        c_copies[ci].start()
    z_copies = {}
    for s in range(1, depth):
        z_copies[0, s] = remote(
            outlet, faces.at[z], z_send.at[0, s - 1], z_recv.at[0, s - 1], column(s)
        )
        z_copies[1, s] = remote(
            merged.at[z], merged.at[z], z_send.at[1, s - 1], z_recv.at[1, s - 1], column(s)
        )
        z_copies[0, s].start()

    consts = spectral_constants(number)

    own_copy.wait()
    lane = lax.broadcasted_iota(jnp.int32, (8, 128), 1)
    group = lax.rem(lane + 2, 128) // 8
    for k in range(6):
        acc = jnp.zeros((8, 128), f32)
        for i in range(8):
            for r in range(2):
                t = 2 * i + r
                acc = jnp.where(group == t, pltpu.roll(own[r, k, 2 + i], (8 * t + 2) % 128, 1), acc)
        pk[k] = acc
    g_copies = [
        remote(pk, pkl, g_send.at[0], g_recv.at[0], (n, bright)),
        remote(pk, pkr, g_send.at[1], g_recv.at[1], (n, bleft)),
    ]
    for c in g_copies:
        c.start()

    first_copy.wait_recv()
    near = (lane >= do_ref[0, 0, 0]) == (lax.rem(db_ref[0, 0, 0], 2) == y)
    for k in range(6):
        for s in range(2):
            merged[z, k, s] = jnp.where(near, own[1, k, 2 + s], yfirst[k, s])
    for s in range(1, depth):
        z_copies[1, s].start()

    for ci in range(RAW, len(chunks)):
        c_copies[ci].wait_recv()
        r, f = chunks[ci]
        for dp in range(1, pairs):
            odd = jnp.where(core == 0, consts[2 * dp - 1], consts[2 * dp + 1])
            for k in range(f, f + GROUP):
                share[dp - 1, r, k] = consts[2 * dp] * own[r, k, 2:10] + odd * buf[partner, r, k]
            x_copies[ci, dp].start()

    lane3 = lax.broadcasted_iota(jnp.int32, (2, 8, 128), 2)
    inner = (lane3 >= 2) & (lane3 < 126)

    def body(i, carry):
        e = [own[:, k, 2 + i] for k in range(6)]
        inverse, pressure, sound = primitives(e)
        inv[:, 2 + i] = inverse
        prs[:, 2 + i] = pressure
        snd[:, 2 + i] = sound
        speeds = (jnp.abs(e[1]) + jnp.abs(e[2]) + jnp.abs(e[3])) * inverse
        step[:, i] = COURANT / (speeds + 3.0 * sound + FREQ * number / 2.0)
        d2 = radial(e, inverse, pressure, sound)
        d3 = circumferential(e, inverse, pressure, sound)
        for k in range(6):
            fx[:, k, i] = d2[k] + jnp.where(inner, d3[k], 0.0)
        return carry

    f_copies = {}

    def forward(ci):
        r, f = chunks[ci]
        for dp in range(1, pairs):
            x_copies[ci, dp].wait_recv()
            slot = lax.rem(pair + pairs - dp, pairs) * 2 + core
            ref = buf.at[slot, r, f : f + GROUP]
            f_copies[dp, ci] = remote(
                ref, ref, f_send.at[dp - 1, ci], f_recv.at[dp - 1, ci], (partner, b)
            )
            f_copies[dp, ci].start()

    lax.fori_loop(0, 8, body, 0)

    for g in range(2):
        own[0, :, g] = own[0, :, 2]
        own[1, :, 10 + g] = own[1, :, 9]
        for ref in (inv, prs, snd):
            ref[0, g] = ref[0, 2]
            ref[1, 10 + g] = ref[1, 9]

    def axial(r, f):
        em, e0, e1, e2 = [[own[r, k, f + s] for k in range(6)] for s in range(4)]
        pm, p0, p1, p2 = [prs[r, f + s] for s in range(4)]
        u0, flux0 = fluxes(e0, 1, inv[r, f + 1], p0)
        u1, flux1 = fluxes(e1, 1, inv[r, f + 2], p1)
        first, fourth = weights_of(
            sensor(pm, p0, p1),
            sensor(p0, p1, p2),
            jnp.abs(u0) + snd[r, f + 1],
            jnp.abs(u1) + snd[r, f + 2],
        )
        for k in range(6):
            hx[r, k, f] = face(flux0[k], flux1[k], first, fourth, em[k], e0[k], e1[k], e2[k])

    def axial_body(f, carry):
        axial(0, f)
        axial(1, f + 2)
        return carry

    lax.fori_loop(0, 7, axial_body, 0)
    for ci in range(RAW):
        forward(ci)

    for c in g_copies:
        c.wait_recv()
    phase = lax.rem(lane, 8)
    strips = []
    for k in range(6):
        mine = pk[k]
        left = jnp.where(phase < 2, pkl[k], mine)
        right = jnp.where((phase >= 2) & (phase < 4), pkr[k], mine)
        strips.append(jnp.stack([left, right]))
    d3 = circumferential(strips, *primitives(strips))
    for k in range(6):
        edge[k] = jnp.where(phase < 2, d3[k][1], d3[k][0])
    outer = (lane < 2) | (lane >= 126)
    for k in range(6):
        both = edge[k]
        for i in range(8):
            for r in range(2):
                shift = (128 - (8 * (2 * i + r) + 2)) % 128
                fx[r, k, i] += jnp.where(outer, pltpu.roll(both, shift, 1), 0.0)

    face_copy.wait()
    for s in range(1, depth):
        z_copies[0, s].wait_recv()
    donor = lax.rem(db_ref[0, 0, 1] + (ypartner - b) + blocks, blocks)
    after = lax.rem(donor + 1, blocks)
    pick = jnp.where(lax.rem(donor, 2) == y, donor // 2, after // 2)
    stage[...] = faces[pick]
    last_copy = remote(stage, ylast, y_send.at[0], y_recv.at[0], (n, ypartner))
    last_copy.start()

    def wait_chunk(ci):
        c_wait = ci < RAW
        for dp in range(1, pairs):
            if c_wait:
                f_copies[dp, ci].wait_recv()
            else:
                x_copies[ci, dp].wait_recv()
        if c_wait:
            c_copies[ci].wait_recv()

    near_weight = jnp.where(core == 0, consts[number - 1], consts[1])

    def time_term(ci, r, k):
        time = consts[0] * own[r, k, 2:10]
        if ci < RAW:
            for q in range(1, number):
                time += consts[q] * buf[lax.rem(n + number - q, number), r, k]
            return time
        time += near_weight * buf[partner, r, k]
        for dp in range(1, pairs):
            time += buf[peer(dp), r, k]
        return time

    def add_time(ci):
        wait_chunk(ci)
        r, f = chunks[ci]
        for k in range(f, f + GROUP):
            fx[r, k] += time_term(ci, r, k)

    for ci in range(RAW):
        add_time(ci)

    def ghosts(row, base, s, cells, shift):
        ghost = []
        for k in range(6):
            ghost.append(pltpu.roll(cells[k], shift, 1))
            own[row, k, base + s] = ghost[k]
        inverse, pressure, sound = primitives(ghost)
        inv[row, base + s] = inverse
        prs[row, base + s] = pressure
        snd[row, base + s] = sound

    def window(row):
        donor = db_ref[0, 0, row]
        offset = do_ref[0, 0, row]
        return donor, lax.rem(donor + 1, blocks), lane >= offset, lax.rem(128 - offset, 128)

    last_copy.wait_recv()
    donor, after, mask, shift = window(1)
    same = lax.rem(donor, 2) == y
    pick = jnp.where(same, donor // 2, after // 2)
    for s in range(2):
        cells = [jnp.where(mask == same, faces[pick, k, s], ylast[k, s]) for k in range(6)]
        ghosts(1, 0, s, cells, shift)
    for s in range(2):
        axial(1, s)

    for s in range(1, depth):
        z_copies[1, s].wait_recv()
    donor, after, mask, shift = window(0)
    for s in range(2):
        cells = [
            jnp.where(mask, merged[donor // 2, k, s], merged[after // 2, k, s]) for k in range(6)
        ]
        ghosts(0, 10, s, cells, shift)
    for s in range(2):
        axial(0, 7 + s)

    for ci, (r, f) in enumerate(chunks):
        if ci >= RAW:
            wait_chunk(ci)
        for k in range(f, f + GROUP):
            total = (hx[r, k, 1:9] - hx[r, k, 0:8]) + fx[r, k]
            if ci >= RAW:
                total += time_term(ci, r, k)
            res_ref[0, r, k] = total
            new_ref[0, r, k] = own[r, k, 2:10] - step[r] * total

    copies = [first_copy, last_copy] + g_copies
    for group_copies in (x_copies, c_copies, f_copies, z_copies):
        copies += list(group_copies.values())
    for c in copies:
        c.wait_send()


def store(res_ref, new_ref, res_out, new_out, sem):
    copies = []
    for r in range(2):
        copies.append(pltpu.make_async_copy(res_ref.at[0, r], res_out.at[0, r], sem.at[0, r]))
        copies.append(pltpu.make_async_copy(new_ref.at[0, r], new_out.at[0, r], sem.at[1, r]))
    for c in copies:
        c.start()
    for c in copies:
        c.wait()


def per_device(number, blocks, state, donor_block, donor_offset):
    pairs, depth = number // 2, blocks // 2
    nch = 2 * (6 // GROUP)
    dma = pltpu.SemaphoreType.DMA
    vmem = lambda *shape: pltpu.VMEM(shape, f32)
    shape = jax.ShapeDtypeStruct(state.shape, f32)
    res, new = pl.pallas_call(
        functools.partial(kernel, number, blocks),
        out_shape=(shape, shape),
        in_specs=[
            pl.BlockSpec(memory_space=pltpu.SMEM),
            pl.BlockSpec(memory_space=pltpu.SMEM),
            pl.BlockSpec(memory_space=pltpu.HBM),
        ],
        out_specs=(
            pl.BlockSpec(memory_space=pltpu.VMEM),
            pl.BlockSpec(memory_space=pltpu.VMEM),
        ),
        scratch_shapes=[
            vmem(2, 6, 12, 8, 128),
            vmem(2, 12, 8, 128),
            vmem(2, 12, 8, 128),
            vmem(2, 12, 8, 128),
            vmem(number, 2, 6, 8, 8, 128),
            vmem(2, 6, 8, 8, 128),
            vmem(2, 6, 9, 8, 128),
            vmem(2, 8, 8, 128),
            vmem(max(pairs - 1, 1), 2, 6, 8, 8, 128),
            vmem(depth, 6, 2, 8, 128),
            vmem(depth, 6, 2, 8, 128),
            vmem(6, 2, 8, 128),
            vmem(6, 2, 8, 128),
            vmem(6, 2, 8, 128),
            vmem(6, 8, 128),
            vmem(6, 8, 128),
            vmem(6, 8, 128),
            vmem(6, 8, 128),
            dma,
            dma,
            dma((pairs, nch)),
            dma((pairs, nch)),
            dma((nch,)),
            dma((nch,)),
            dma((pairs, nch)),
            dma((pairs, nch)),
            dma((2, depth)),
            dma((2, depth)),
            dma((2,)),
            dma((2,)),
            dma((2,)),
            dma((2,)),
        ],
        compiler_params=pltpu.CompilerParams(
            collective_id=0, has_side_effects=True, vmem_limit_bytes=32 * 1024 * 1024
        ),
    )(jnp.transpose(donor_block, (0, 2, 1)), jnp.transpose(donor_offset, (0, 2, 1)), state)
    return pl.pallas_call(
        store,
        out_shape=(shape, shape),
        in_specs=[pl.BlockSpec(memory_space=pl.ANY)] * 2,
        out_specs=(pl.BlockSpec(memory_space=pl.ANY), pl.BlockSpec(memory_space=pl.ANY)),
        scratch_shapes=[dma((2, 2))],
        compiler_params=pltpu.CompilerParams(vmem_limit_bytes=1024 * 1024),
    )(res, new)


def solution(mesh):
    number, blocks = mesh.shape["inst"], mesh.shape["blk"]
    return jax.shard_map(
        functools.partial(per_device, number, blocks),
        mesh=mesh,
        in_specs=(
            P("inst", None, None, None, None, "blk"),
            P("inst", None, "blk"),
            P("inst", None, "blk"),
        ),
        out_specs=(
            P("inst", None, None, None, None, "blk"),
            P("inst", None, None, None, None, "blk"),
        ),
        check_vma=False,
    )
```

```python
import functools
import math

import jax
import jax.numpy as jnp
from jax import lax
from jax.experimental import pallas as pl
from jax.experimental.pallas import tpu as pltpu
from jax.sharding import PartitionSpec as P

GAMMA = 1.4
K2 = 0.5
K4 = 1.0 / 32.0
COURANT = 0.8
FREQ = 0.5
GROUP = 3
RAW = 1
MESH = pl.DeviceIdType.MESH
f32 = jnp.float32


def spectral_constants(number):
    out = []
    for r in range(number):
        cot = 0.0 if r == 0 else math.cos(math.pi * r / number) / math.sin(math.pi * r / number)
        out.append((-1.0) ** r * (0.25 * FREQ + 0.5 * FREQ * cot))
    return out


def primitives(e):
    inverse = 1.0 / e[0]
    kinetic = 0.5 * (e[1] * e[1] + e[2] * e[2] + e[3] * e[3]) * inverse
    pressure = (GAMMA - 1.0) * (e[4] - kinetic)
    sound = jnp.sqrt(GAMMA * pressure * inverse)
    return inverse, pressure, sound


def fluxes(e, a, inverse, pressure):
    u = e[a] * inverse
    out = [e[a]]
    for k in (1, 2, 3):
        out.append(e[k] * u + pressure if k == a else e[k] * u)
    return u, out + [(e[4] + pressure) * u, e[5] * u]


def sensor(minus, here, plus):
    total = plus + minus
    return jnp.abs(total - 2.0 * here) / (total + 2.0 * here)


def weights_of(nu0, nu1, lam0, lam1):
    spread = 0.5 * (lam0 + lam1)
    eps2 = K2 * jnp.maximum(nu0, nu1)
    eps4 = jnp.maximum(0.0, K4 - eps2)
    fourth = spread * eps4
    return spread * eps2 + 3.0 * fourth, fourth


def face(flux0, flux1, first, fourth, em, e0, e1, e2):
    return 0.5 * (flux0 + flux1) - first * (e1 - e0) + fourth * (e2 - em)


def circumferential(e, inverse, pressure, sound):
    axis = e[0].ndim - 1

    def nxt(v):
        return pltpu.roll(v, 127, axis)

    def prv(v):
        return pltpu.roll(v, 1, axis)

    u, flux = fluxes(e, 3, inverse, pressure)
    lam = jnp.abs(u) + sound
    nu = sensor(prv(pressure), pressure, nxt(pressure))
    first, fourth = weights_of(nu, nxt(nu), lam, nxt(lam))
    out = []
    for k in range(6):
        e1 = nxt(e[k])
        h = face(flux[k], nxt(flux[k]), first, fourth, prv(e[k]), e[k], e1, nxt(e1))
        out.append(h - prv(h))
    return out


def radial(e, inverse, pressure, sound):
    axis = e[0].ndim - 2
    row = lax.broadcasted_iota(jnp.int32, e[0].shape, axis)
    top, bottom = row == 7, row == 0

    def nxt(v, s=1.0):
        return jnp.where(top, v if s > 0 else -v, pltpu.roll(v, 7, axis))

    def prv(v, s=1.0):
        return jnp.where(bottom, v if s > 0 else -v, pltpu.roll(v, 1, axis))

    u, flux = fluxes(e, 2, inverse, pressure)
    lam = jnp.abs(u) + sound
    nu = sensor(prv(pressure), pressure, nxt(pressure))
    first, fourth = weights_of(nu, nxt(nu), lam, nxt(lam))
    out = []
    for k in range(6):
        s = -1.0 if k == 2 else 1.0
        e1 = nxt(e[k], s)
        em = prv(e[k], s)
        e2 = jnp.where(top, em if s > 0 else -em, pltpu.roll(e1, 7, axis))
        h = face(flux[k], nxt(flux[k], -s), first, fourth, em, e[k], e1, e2)
        if k == 2:
            eps2 = K2 * nu
            eps4 = jnp.maximum(0.0, K4 - eps2)
            wall = flux[2] - lam * (eps2 * (2.0 * e[2]) - eps4 * (2.0 * e1 - 6.0 * e[2]))
        else:
            wall = jnp.zeros_like(h)
        out.append(h - jnp.where(bottom, wall, pltpu.roll(h, 1, axis)))
    return out


def kernel(
    number,
    blocks,
    db_any,
    do_any,
    st_ref,
    res_ref,
    new_ref,
    db_ref,
    do_ref,
    donor_sem,
    own,
    inv,
    prs,
    snd,
    buf,
    fx,
    hx,
    step,
    share,
    faces,
    merged,
    stage,
    yfirst,
    ylast,
    pk,
    pkl,
    pkr,
    edge,
    own_sem,
    face_sem,
    x_send,
    x_recv,
    c_send,
    c_recv,
    f_send,
    f_recv,
    z_send,
    z_recv,
    y_send,
    y_recv,
    g_send,
    g_recv,
):
    n = lax.axis_index("inst")
    b = lax.axis_index("blk")
    pairs = number // 2
    depth = blocks // 2
    pair, core = n // 2, n % 2
    z, y = b // 2, b % 2
    partner = n + 1 - 2 * core
    ypartner = b + 1 - 2 * y
    bright = lax.rem(b + 1, blocks)
    bleft = lax.rem(b + blocks - 1, blocks)
    chunks = [(r, f) for r in range(2) for f in range(0, 6, GROUP)]

    def peer(dp):
        return lax.rem(pair + dp, pairs) * 2 + core

    outlet = st_ref.at[0, 0, :, 6:8]
    inlet = st_ref.at[0, 1, :, 0:2]
    def column(s):
        return (n, lax.rem(z + s, depth) * 2 + y)

    barrier = pltpu.get_barrier_semaphore()
    greet = [(peer(dp), b) for dp in range(1, pairs)]
    greet += [(partner, b), (n, ypartner), (n, bright), (n, bleft)]
    greet += [column(s) for s in range(1, depth)]
    for target in greet:
        pl.semaphore_signal(barrier, inc=1, device_id=target, device_id_type=MESH)
    own_copy = pltpu.make_async_copy(st_ref.at[0], own.at[:, :, 2:10], own_sem)
    own_copy.start()
    face_copy = pltpu.make_async_copy(outlet, faces.at[z], face_sem)
    face_copy.start()
    donor_copies = [
        pltpu.make_async_copy(db_any, db_ref, donor_sem.at[0]),
        pltpu.make_async_copy(do_any, do_ref, donor_sem.at[1]),
    ]
    for c in donor_copies:
        c.start()
    pl.semaphore_wait(barrier, len(greet))

    def remote(src, dst, ss, rs, target):
        return pltpu.make_async_remote_copy(
            src_ref=src, dst_ref=dst, send_sem=ss, recv_sem=rs, device_id=target, device_id_type=MESH
        )

    x_copies, c_copies = {}, {}
    for ci, (r, f) in enumerate(chunks):
        part = (r, slice(f, f + GROUP))
        for dp in range(1, pairs):
            src = st_ref.at[(0, *part)] if ci < RAW else share.at[(dp - 1, *part)]
            x_copies[ci, dp] = remote(
                src,
                buf.at[(n, *part)],
                x_send.at[dp - 1, ci],
                x_recv.at[dp - 1, ci],
                (peer(dp), b),
            )
        c_copies[ci] = remote(
            st_ref.at[(0, *part)], buf.at[(n, *part)], c_send.at[ci], c_recv.at[ci], (partner, b)
        )
    for ci in range(RAW):
        for dp in range(1, pairs):
            x_copies[ci, dp].start()
    first_copy = remote(inlet, yfirst, y_send.at[1], y_recv.at[1], (n, ypartner))
    first_copy.start()
    for ci in list(range(RAW, len(chunks))) + list(range(RAW)):
        c_copies[ci].start()
    z_copies = {}
    for s in range(1, depth):
        z_copies[0, s] = remote(
            outlet, faces.at[z], z_send.at[0, s - 1], z_recv.at[0, s - 1], column(s)
        )
        z_copies[1, s] = remote(
            merged.at[z], merged.at[z], z_send.at[1, s - 1], z_recv.at[1, s - 1], column(s)
        )
        z_copies[0, s].start()

    consts = spectral_constants(number)

    own_copy.wait()
    for ci in range(RAW, len(chunks)):
        c_copies[ci].wait_recv()
        r, f = chunks[ci]
        for dp in range(1, pairs):
            odd = jnp.where(core == 0, consts[2 * dp - 1], consts[2 * dp + 1])
            for k in range(f, f + GROUP):
                share[dp - 1, r, k] = consts[2 * dp] * own[r, k, 2:10] + odd * buf[partner, r, k]
            x_copies[ci, dp].start()

    lane = lax.broadcasted_iota(jnp.int32, (8, 128), 1)
    group = lax.rem(lane + 2, 128) // 8
    for k in range(6):
        acc = jnp.zeros((8, 128), f32)
        for i in range(8):
            for r in range(2):
                t = 2 * i + r
                acc = jnp.where(group == t, pltpu.roll(own[r, k, 2 + i], (8 * t + 2) % 128, 1), acc)
        pk[k] = acc
    g_copies = [
        remote(pk, pkl, g_send.at[0], g_recv.at[0], (n, bright)),
        remote(pk, pkr, g_send.at[1], g_recv.at[1], (n, bleft)),
    ]
    for c in g_copies:
        c.start()

    for c in donor_copies:
        c.wait()
    first_copy.wait_recv()
    near = (lane >= do_ref[0, 0, 0]) == (lax.rem(db_ref[0, 0, 0], 2) == y)
    for k in range(6):
        for s in range(2):
            merged[z, k, s] = jnp.where(near, own[1, k, 2 + s], yfirst[k, s])
    for s in range(1, depth):
        z_copies[1, s].start()

    lane3 = lax.broadcasted_iota(jnp.int32, (2, 8, 128), 2)
    inner = (lane3 >= 2) & (lane3 < 126)

    def body(i, carry):
        e = [own[:, k, 2 + i] for k in range(6)]
        inverse, pressure, sound = primitives(e)
        inv[:, 2 + i] = inverse
        prs[:, 2 + i] = pressure
        snd[:, 2 + i] = sound
        speeds = (jnp.abs(e[1]) + jnp.abs(e[2]) + jnp.abs(e[3])) * inverse
        step[:, i] = COURANT / (speeds + 3.0 * sound + FREQ * number / 2.0)
        d2 = radial(e, inverse, pressure, sound)
        d3 = circumferential(e, inverse, pressure, sound)
        for k in range(6):
            fx[:, k, i] = d2[k] + jnp.where(inner, d3[k], 0.0)
        return carry

    f_copies = {}

    def forward(ci):
        r, f = chunks[ci]
        for dp in range(1, pairs):
            x_copies[ci, dp].wait_recv()
            slot = lax.rem(pair + pairs - dp, pairs) * 2 + core
            ref = buf.at[slot, r, f : f + GROUP]
            f_copies[dp, ci] = remote(
                ref, ref, f_send.at[dp - 1, ci], f_recv.at[dp - 1, ci], (partner, b)
            )
            f_copies[dp, ci].start()

    lax.fori_loop(0, 8, body, 0)

    for g in range(2):
        own[0, :, g] = own[0, :, 2]
        own[1, :, 10 + g] = own[1, :, 9]
        for ref in (inv, prs, snd):
            ref[0, g] = ref[0, 2]
            ref[1, 10 + g] = ref[1, 9]

    def axial(r, f):
        em, e0, e1, e2 = [[own[r, k, f + s] for k in range(6)] for s in range(4)]
        pm, p0, p1, p2 = [prs[r, f + s] for s in range(4)]
        u0, flux0 = fluxes(e0, 1, inv[r, f + 1], p0)
        u1, flux1 = fluxes(e1, 1, inv[r, f + 2], p1)
        first, fourth = weights_of(
            sensor(pm, p0, p1),
            sensor(p0, p1, p2),
            jnp.abs(u0) + snd[r, f + 1],
            jnp.abs(u1) + snd[r, f + 2],
        )
        for k in range(6):
            hx[r, k, f] = face(flux0[k], flux1[k], first, fourth, em[k], e0[k], e1[k], e2[k])

    def axial_body(f, carry):
        axial(0, f)
        axial(1, f + 2)
        return carry

    lax.fori_loop(0, 7, axial_body, 0)
    for ci in range(RAW):
        forward(ci)

    for c in g_copies:
        c.wait_recv()
    phase = lax.rem(lane, 8)
    strips = []
    for k in range(6):
        mine = pk[k]
        left = jnp.where(phase < 2, pkl[k], mine)
        right = jnp.where((phase >= 2) & (phase < 4), pkr[k], mine)
        strips.append(jnp.stack([left, right]))
    d3 = circumferential(strips, *primitives(strips))
    for k in range(6):
        edge[k] = jnp.where(phase < 2, d3[k][1], d3[k][0])
    outer = (lane < 2) | (lane >= 126)
    for k in range(6):
        both = edge[k]
        for i in range(8):
            for r in range(2):
                shift = (128 - (8 * (2 * i + r) + 2)) % 128
                fx[r, k, i] += jnp.where(outer, pltpu.roll(both, shift, 1), 0.0)

    face_copy.wait()
    for s in range(1, depth):
        z_copies[0, s].wait_recv()
    donor = lax.rem(db_ref[0, 0, 1] + (ypartner - b) + blocks, blocks)
    after = lax.rem(donor + 1, blocks)
    pick = jnp.where(lax.rem(donor, 2) == y, donor // 2, after // 2)
    stage[...] = faces[pick]
    last_copy = remote(stage, ylast, y_send.at[0], y_recv.at[0], (n, ypartner))
    last_copy.start()

    def wait_chunk(ci):
        c_wait = ci < RAW
        for dp in range(1, pairs):
            if c_wait:
                f_copies[dp, ci].wait_recv()
            else:
                x_copies[ci, dp].wait_recv()
        if c_wait:
            c_copies[ci].wait_recv()

    near_weight = jnp.where(core == 0, consts[number - 1], consts[1])

    def time_term(ci, r, k):
        time = consts[0] * own[r, k, 2:10]
        if ci < RAW:
            for q in range(1, number):
                time += consts[q] * buf[lax.rem(n + number - q, number), r, k]
            return time
        time += near_weight * buf[partner, r, k]
        for dp in range(1, pairs):
            time += buf[peer(dp), r, k]
        return time

    def add_time(ci):
        wait_chunk(ci)
        r, f = chunks[ci]
        for k in range(f, f + GROUP):
            fx[r, k] += time_term(ci, r, k)

    for ci in range(RAW):
        add_time(ci)

    def ghosts(row, base, s, cells, shift):
        ghost = []
        for k in range(6):
            ghost.append(pltpu.roll(cells[k], shift, 1))
            own[row, k, base + s] = ghost[k]
        inverse, pressure, sound = primitives(ghost)
        inv[row, base + s] = inverse
        prs[row, base + s] = pressure
        snd[row, base + s] = sound

    def window(row):
        donor = db_ref[0, 0, row]
        offset = do_ref[0, 0, row]
        return donor, lax.rem(donor + 1, blocks), lane >= offset, lax.rem(128 - offset, 128)

    last_copy.wait_recv()
    donor, after, mask, shift = window(1)
    same = lax.rem(donor, 2) == y
    pick = jnp.where(same, donor // 2, after // 2)
    for s in range(2):
        cells = [jnp.where(mask == same, faces[pick, k, s], ylast[k, s]) for k in range(6)]
        ghosts(1, 0, s, cells, shift)
    for s in range(2):
        axial(1, s)

    for s in range(1, depth):
        z_copies[1, s].wait_recv()
    donor, after, mask, shift = window(0)
    for s in range(2):
        cells = [
            jnp.where(mask, merged[donor // 2, k, s], merged[after // 2, k, s]) for k in range(6)
        ]
        ghosts(0, 10, s, cells, shift)
    for s in range(2):
        axial(0, 7 + s)

    for ci, (r, f) in enumerate(chunks):
        if ci >= RAW:
            wait_chunk(ci)
        for k in range(f, f + GROUP):
            total = (hx[r, k, 1:9] - hx[r, k, 0:8]) + fx[r, k]
            if ci >= RAW:
                total += time_term(ci, r, k)
            res_ref[0, r, k] = total
            new_ref[0, r, k] = own[r, k, 2:10] - step[r] * total

    copies = [first_copy, last_copy] + g_copies
    for group_copies in (x_copies, c_copies, f_copies, z_copies):
        copies += list(group_copies.values())
    for c in copies:
        c.wait_send()


def store(res_ref, new_ref, res_out, new_out, sem):
    copies = []
    for r in range(2):
        copies.append(pltpu.make_async_copy(res_ref.at[0, r], res_out.at[0, r], sem.at[0, r]))
        copies.append(pltpu.make_async_copy(new_ref.at[0, r], new_out.at[0, r], sem.at[1, r]))
    for c in copies:
        c.start()
    for c in copies:
        c.wait()


def per_device(number, blocks, state, donor_block, donor_offset):
    pairs, depth = number // 2, blocks // 2
    nch = 2 * (6 // GROUP)
    dma = pltpu.SemaphoreType.DMA
    vmem = lambda *shape: pltpu.VMEM(shape, f32)
    shape = jax.ShapeDtypeStruct(state.shape, f32)
    res, new = pl.pallas_call(
        functools.partial(kernel, number, blocks),
        out_shape=(shape, shape),
        in_specs=[
            pl.BlockSpec(memory_space=pl.ANY),
            pl.BlockSpec(memory_space=pl.ANY),
            pl.BlockSpec(memory_space=pl.ANY),
        ],
        out_specs=(
            pl.BlockSpec(memory_space=pltpu.VMEM),
            pl.BlockSpec(memory_space=pltpu.VMEM),
        ),
        scratch_shapes=[
            pltpu.SMEM((1, 1, 2), jnp.int32),
            pltpu.SMEM((1, 1, 2), jnp.int32),
            dma((2,)),
            vmem(2, 6, 12, 8, 128),
            vmem(2, 12, 8, 128),
            vmem(2, 12, 8, 128),
            vmem(2, 12, 8, 128),
            vmem(number, 2, 6, 8, 8, 128),
            vmem(2, 6, 8, 8, 128),
            vmem(2, 6, 9, 8, 128),
            vmem(2, 8, 8, 128),
            vmem(max(pairs - 1, 1), 2, 6, 8, 8, 128),
            vmem(depth, 6, 2, 8, 128),
            vmem(depth, 6, 2, 8, 128),
            vmem(6, 2, 8, 128),
            vmem(6, 2, 8, 128),
            vmem(6, 2, 8, 128),
            vmem(6, 8, 128),
            vmem(6, 8, 128),
            vmem(6, 8, 128),
            vmem(6, 8, 128),
            dma,
            dma,
            dma((pairs, nch)),
            dma((pairs, nch)),
            dma((nch,)),
            dma((nch,)),
            dma((pairs, nch)),
            dma((pairs, nch)),
            dma((2, depth)),
            dma((2, depth)),
            dma((2,)),
            dma((2,)),
            dma((2,)),
            dma((2,)),
        ],
        compiler_params=pltpu.CompilerParams(
            collective_id=0, has_side_effects=True, vmem_limit_bytes=53 * 1024 * 1024
        ),
    )(jnp.transpose(donor_block, (0, 2, 1)), jnp.transpose(donor_offset, (0, 2, 1)), state)
    return pl.pallas_call(
        store,
        out_shape=(shape, shape),
        in_specs=[pl.BlockSpec(memory_space=pl.ANY)] * 2,
        out_specs=(pl.BlockSpec(memory_space=pl.ANY), pl.BlockSpec(memory_space=pl.ANY)),
        scratch_shapes=[dma((2, 2))],
        compiler_params=pltpu.CompilerParams(vmem_limit_bytes=1024 * 1024),
    )(res, new)


def solution(mesh):
    number, blocks = mesh.shape["inst"], mesh.shape["blk"]
    return jax.shard_map(
        functools.partial(per_device, number, blocks),
        mesh=mesh,
        in_specs=(
            P("inst", None, None, None, None, "blk"),
            P("inst", None, "blk"),
            P("inst", None, "blk"),
        ),
        out_specs=(
            P("inst", None, None, None, None, "blk"),
            P("inst", None, None, None, None, "blk"),
        ),
        check_vma=False,
    )
```
